32 devices in a mesh: grp: 4 (over y, core), tile: 8 (over z, x).
Axes of the slice: x: 2, y: 2, z: 4, core: 2. Of those that a mesh axis runs over, the one named last changes fastest.
Arguments:
- material: int32 [6, 1536, 2048], P(None, 'grp', 'tile'), may hold values from 0 to 7
- conduct_table: float32 [8], replicated, may hold values from 1 to 20
- heat_sink: float32 [1536, 2048], P('grp', 'tile'), may hold values from 1 to 10
- heat_source: float32 [6, 1536, 2048], P(None, 'grp', 'tile'), may hold values from -120 to 120
- die_power: float32 [192, 128, 128], P(('grp', 'tile')), may hold values from -60 to 60
- die_conduct: float32 [192], P(('grp', 'tile')), may hold values from 1 to 8
- bond_conductance: float32 [192], P(('grp', 'tile')), may hold values from 0.5 to 4
- tile_place: int32 [192], P(('grp', 'tile')), may hold values from -1 to 191, as said below
Outputs:
- interposer_temp: float32 [6, 1536, 2048], P(None, 'grp', 'tile')
- die_temp: float32 [192, 128, 128], P(('grp', 'tile'))
The draws below stay inside these ranges and needn't reach their ends.
Inputs may be any that keep to these rules, and one draw needn't show every extreme that they name: `tile_place`: -1 marks an empty slot; the other entries are distinct tile positions; one device holds all 6 of its slots filled and every device at least one.
All inputs are finite; a program needn't handle non-finite values.
Results may differ from the reference program's by a relative error of at most 0.0003.
Values sent between devices are 32-bit elements; how exact they have to be, the bound alone decides.
A program may use at most 192 MiB of HBM per device.

```python
import math
import jax
import jax.numpy as jnp

LAYERS = 6
MATS = 8
TS = 128
RATIO = 8
NU = 2
NC = 4
TILE_DEV = 6
TILES = 192
NX = 1536
NY = 2048


def draw_tile_place(key, part):
    device_count = TILES // TILE_DEV
    keys = jax.random.split(jax.random.fold_in(key, 17), 5)
    full_device = jax.random.randint(keys[0], (), 0, device_count)
    counts = 1 + jax.random.randint(keys[1], (device_count,), 0, TILE_DEV // 2)
    counts = jnp.where(jnp.arange(device_count) == full_device, TILE_DEV, counts)
    scores = jax.random.randint(keys[2], (device_count, TILE_DEV), 0, 1 << 20) * TILE_DEV + jnp.arange(TILE_DEV)[None, :]
    rank_local = jnp.argsort(jnp.argsort(scores, axis=1), axis=1)
    filled = (rank_local < counts[:, None]).reshape(TILES)
    slot_keys = jnp.where(filled, 0, 1) * TILES + jax.random.permutation(keys[3], TILES)
    slot_order = jnp.argsort(slot_keys)
    position_order = jax.random.permutation(keys[4], TILES)
    total = jnp.sum(filled.astype(jnp.int32))
    placed = jnp.where(jnp.arange(TILES) < total, position_order, -1).astype(jnp.int32)
    return jnp.zeros((TILES,), jnp.int32).at[slot_order].set(placed).astype(jnp.int32)


def with_ends(array, own_key, low, largest):
    longest = array.shape.index(max(array.shape))
    spots = []
    for shift in (0, 1):
        where = [jax.random.randint(jax.random.fold_in(own_key, axis), (), 0, length) for axis, length in enumerate(array.shape)]
        where[longest] = (where[longest] + shift) % array.shape[longest]
        spots.append(tuple(where))
    return array.at[spots[0]].set(low).at[spots[1]].set(largest)


def steps_of(stream_key, dims, pieces, least, top_value):
    def one(dim, shards_of):
        heights = jax.random.uniform(jax.random.fold_in(jax.random.fold_in(stream_key, 6), dim), (shards_of,), jnp.float32, least / len(pieces), top_value / len(pieces))
        return jnp.repeat(jnp.exp(heights), dims[dim] // shards_of).reshape((-1,) + (1,) * (len(dims) - dim - 1))

    level = one(*pieces[0])
    for cut in pieces[1:]:
        level = level * one(*cut)
    return level


def normal_values(stream_key, dims, width, bound, cuts=(), kind=jnp.bfloat16):
    level = steps_of(stream_key, dims, cuts, -0.22, 0.18) if cuts else 1.0
    values = jax.random.normal(stream_key, dims, jnp.float32) * width * level
    return jnp.minimum(jnp.maximum(values, -bound), bound).astype(kind)


def setup_inputs(seed: int = 0) -> dict:
    key_list = jax.random.split(jax.random.key(seed), 9)
    return {
        "material": with_ends(jax.random.randint(key_list[0], (LAYERS, NX, NY), 0, MATS), jax.random.fold_in(key_list[0], 1), 0, MATS - 1).astype(jnp.int32),
        "conduct_table": jnp.clip(jnp.exp(jax.random.uniform(key_list[1], (MATS,), jnp.float32, math.log(1.0), math.log(20.0))), 1.0, 20.0),
        "heat_sink": jnp.clip(jnp.exp(math.log(10.0) - 2.3025851 * jax.random.uniform(key_list[2], (NX, NY), jnp.float32) ** steps_of(key_list[2], (NX, NY), ((0, 4), (1, 8)), -0.2, 0.2)), 1.0, 10.0),
        "heat_source": normal_values(key_list[3], (LAYERS, NX, NY), 20.0, 120.0, ((1, 4), (2, 8)), jnp.float32),
        "die_power": normal_values(key_list[4], (TILES, TS, TS), 10.0, 60.0, ((0, 32),), jnp.float32),
        "die_conduct": jnp.clip(jnp.exp(math.log(8.0) - 2.0794415 * jax.random.uniform(key_list[5], (TILES,), jnp.float32) ** steps_of(key_list[5], (TILES,), ((0, 32),), -0.2, 0.2)), 1.0, 8.0),
        "bond_conductance": jnp.clip(jnp.exp(math.log(4.0) - 2.0794415 * jax.random.uniform(key_list[6], (TILES,), jnp.float32) ** steps_of(key_list[6], (TILES,), ((0, 32),), -0.2, 0.2)), 0.5, 4.0),
        "tile_place": draw_tile_place(jax.random.fold_in(key_list[8], 71), 0),
    }


relax_weight = 0.8


def harmonic(lower_side, upper_side):
    total = lower_side + upper_side
    return 2.0 * lower_side * upper_side / jnp.where(total > 0, total, 1.0)


def neighbours(padded):
    return (padded[:-2, 1:-1, 1:-1], padded[2:, 1:-1, 1:-1], padded[1:-1, :-2, 1:-1],
            padded[1:-1, 2:, 1:-1], padded[1:-1, 1:-1, :-2], padded[1:-1, 1:-1, 2:])


def grid_faces(padded, vertical):
    centre = padded[1:-1, 1:-1, 1:-1]
    scales = (vertical, vertical, 1.0, 1.0, 1.0, 1.0)
    return tuple(harmonic(centre, other) * weight_value for other, weight_value in zip(neighbours(padded), scales))


def grid_residual(padded, faces, extra, source):
    centre = padded[1:-1, 1:-1, 1:-1]
    flux_sum = extra * centre
    diagonal = extra
    for face, other in zip(faces, neighbours(padded)):
        flux_sum = flux_sum + face * (centre - other)
        diagonal = diagonal + face
    return source - flux_sum, diagonal


def grid_sweep(padded, faces, extra, source):
    residual_part, diagonal = grid_residual(padded, faces, extra, source)
    centre = padded[1:-1, 1:-1, 1:-1]
    return centre + relax_weight * residual_part / jnp.where(diagonal > 0, diagonal, 1.0)


def in_block(length, block_size, offset):
    relative = (jnp.arange(length) - offset) % block_size
    return (relative != 0).astype(jnp.float32), (relative != block_size - 1).astype(jnp.float32)


def die_faces(conduct, block_size, offset):
    lower_x, upper_x = in_block(conduct.shape[-2], block_size, offset)
    lower_y, upper_y = in_block(conduct.shape[-1], block_size, offset)
    return (conduct * lower_x[:, None], conduct * upper_x[:, None], conduct * lower_y[None, :], conduct * upper_y[None, :])


def die_residual(field, faces, couple, top_field, source):
    widths = [(0, 0)] * (field.ndim - 2) + [(1, 1), (1, 1)]
    padded = jnp.pad(field, widths)
    views = (padded[..., :-2, 1:-1], padded[..., 2:, 1:-1], padded[..., 1:-1, :-2], padded[..., 1:-1, 2:])
    flux_sum = couple * field
    diagonal = couple
    for face, other in zip(faces, views):
        flux_sum = flux_sum + face * (field - other)
        diagonal = diagonal + face
    return source + couple * top_field - flux_sum, diagonal


def die_sweep(field, faces, couple, top_field, source):
    residual_part, diagonal = die_residual(field, faces, couple, top_field, source)
    return field + relax_weight * residual_part / jnp.where(diagonal > 0, diagonal, 1.0)


def coarsen(field, factor):
    shape = field.shape
    split = field.reshape(shape[:-2] + (shape[-2] // factor, factor, shape[-1] // factor, factor))
    return split.sum(axis=(-3, -1))


def refine(field, factor):
    return jnp.repeat(jnp.repeat(field, factor, axis=-2), factor, axis=-1)


def on_layers(bottom, top_layer, layer_count):
    middle = jnp.zeros((layer_count - 2,) + bottom.shape, jnp.float32)
    return jnp.concatenate([bottom[None], middle, top_layer[None]], 0)


def cell_conduct(material, conduct_table):
    values = jnp.zeros(material.shape, jnp.float32)
    for kind in range(conduct_table.shape[0]):
        values = values + jnp.where(material == kind, conduct_table[kind], 0.0)
    return values


def blocks_to_field(blocks, blocks_down, blocks_across):
    edge_cells = blocks.shape[-1]
    shaped = blocks.reshape(blocks_down, blocks_across, edge_cells, edge_cells)
    return shaped.transpose(0, 2, 1, 3).reshape(blocks_down * edge_cells, blocks_across * edge_cells)


def field_to_blocks(field, blocks_down, blocks_across, edge_cells):
    shaped = field.reshape(blocks_down, edge_cells, blocks_across, edge_cells)
    return shaped.transpose(0, 2, 1, 3).reshape(blocks_down * blocks_across, edge_cells, edge_cells)


def reference(material, conduct_table, heat_sink, heat_source, die_power, die_conduct, bond_conductance, tile_place):
    layer_count, row_count, col_count = material.shape
    block_edge = die_power.shape[1]
    coarse_block = block_edge // RATIO
    blocks_down = row_count // block_edge
    blocks_across = col_count // block_edge
    area = float(RATIO * RATIO)
    cell_values = cell_conduct(material, conduct_table)
    fine_faces = grid_faces(jnp.pad(cell_values, 1), 1.0)
    fine_extra = on_layers(heat_sink, jnp.zeros_like(heat_sink), layer_count)
    interposer = jnp.zeros_like(heat_source)
    for repeat_index in range(NU):
        interposer = grid_sweep(jnp.pad(interposer, 1), fine_faces, fine_extra, heat_source)
    fine_resid = grid_residual(jnp.pad(interposer, 1), fine_faces, fine_extra, heat_source)[0]

    filled = (tile_place >= 0).astype(jnp.float32)
    ones_block = jnp.ones((1, block_edge, block_edge), jnp.float32)
    slot_faces = die_faces(die_conduct[:, None, None] * ones_block, block_edge, 0)
    slot_couple = bond_conductance[:, None, None] * ones_block
    zero_top = jnp.zeros_like(die_power)
    die_field = jnp.zeros_like(die_power)
    for repeat_index in range(NU):
        die_field = die_sweep(die_field, slot_faces, slot_couple, zero_top, die_power)
    die_resid = die_residual(die_field, slot_faces, slot_couple, zero_top, die_power)[0] * filled[:, None, None]

    coarse_rhs = coarsen(fine_resid, RATIO)
    die_coarse = coarsen(die_resid, RATIO)
    index_safe = jnp.maximum(tile_place, 0).astype(jnp.int32)
    pos_rhs = jnp.zeros_like(die_coarse).at[index_safe].add(die_coarse)
    pos_conduct = jnp.zeros(tile_place.shape, jnp.float32).at[index_safe].add(die_conduct * filled)
    pos_couple = jnp.zeros(tile_place.shape, jnp.float32).at[index_safe].add(bond_conductance * area * filled)
    coarse_ones = jnp.ones((1, coarse_block, coarse_block), jnp.float32)
    top_rhs = blocks_to_field(pos_rhs, blocks_down, blocks_across)
    top_conduct = blocks_to_field(pos_conduct[:, None, None] * coarse_ones, blocks_down, blocks_across)
    top_couple = blocks_to_field(pos_couple[:, None, None] * coarse_ones, blocks_down, blocks_across)

    coarse_k = coarsen(cell_values, RATIO) / area
    coarse_sink = coarsen(heat_sink, RATIO)
    coarse_faces = grid_faces(jnp.pad(coarse_k, 1), area)
    top_faces = die_faces(top_conduct, coarse_block, 0)
    coarse_extra = on_layers(coarse_sink, top_couple, layer_count)
    coarse_error = jnp.zeros_like(coarse_rhs)
    top_error = jnp.zeros_like(top_rhs)
    for repeat_index in range(NC):
        pull_term = on_layers(jnp.zeros_like(coarse_sink), top_couple * top_error, layer_count)
        next_error = grid_sweep(jnp.pad(coarse_error, 1), coarse_faces, coarse_extra, coarse_rhs + pull_term)
        top_error = die_sweep(top_error, top_faces, top_couple, coarse_error[-1], top_rhs)
        coarse_error = next_error

    interposer = interposer + refine(coarse_error, RATIO)
    slot_error = field_to_blocks(top_error, blocks_down, blocks_across, coarse_block)[index_safe] * filled[:, None, None]
    die_field = die_field + refine(slot_error, RATIO)
    for repeat_index in range(NU):
        interposer = grid_sweep(jnp.pad(interposer, 1), fine_faces, fine_extra, heat_source)
    for repeat_index in range(NU):
        die_field = die_sweep(die_field, slot_faces, slot_couple, zero_top, die_power)
    return interposer, die_field * filled[:, None, None]
```

```python
import functools
import jax
import jax.numpy as jnp
from jax import lax
from jax.experimental import pallas as pl
from jax.experimental.pallas import tpu as pltpu
from jax.sharding import PartitionSpec as P

RATIO = 8
NU = 2
NC = 4
RELAX = 0.8
HALO = 4
TOP = 16
LANES = 128
MESH = pl.DeviceIdType.MESH
HIGHEST = lax.Precision.HIGHEST
DIRECTIONS = ((-1, 0), (1, 0), (0, -1), (0, 1), (-1, -1), (-1, 1), (1, -1), (1, 1))


def inverse(x):
    r = pl.reciprocal(x, approx=True)
    return r * (2.0 - x * r)


def harmonic(a, b):
    total = a + b
    return 2.0 * a * b * inverse(jnp.where(total > 0, total, 1.0))


def guarded_weight(d):
    return RELAX * inverse(jnp.where(d > 0, d, 1.0))


def iota(shape, dim):
    return lax.broadcasted_iota(jnp.int32, shape, dim)


def shift(x, amount, axis):
    return pltpu.roll(x, amount % x.shape[axis], axis)


def rows_at(ref, l, r, offset):
    if offset < 0:
        return ref.at[l, pl.ds(pl.multiple_of(r - 8, 8), 16), :][8 + offset : 16 + offset, :]
    return ref.at[l, pl.ds(r, 16), :][offset : 8 + offset, :]


def dot(a, b):
    return jnp.dot(a, b, precision=HIGHEST, preferred_element_type=jnp.float32)


def kernel(
    grp_count,
    tile_count,
    material,
    table,
    heat_sink,
    source,
    die_power,
    die_conduct,
    bond,
    place,
    out,
    die_out,
    field,
    zx,
    zy,
    zz,
    diag,
    weight,
    ua,
    ub,
    packed,
    turned,
    from_side,
    from_corner,
    sums,
    rough,
    rough_side,
    rough_row,
    rough_corner,
    dies,
    die_message,
    all_dies,
    die_fix,
    all_fixes,
    wide,
    solved,
    spread,
    send_sem,
    recv_sem,
    gather_send,
    gather_recv,
):
    layers, rows, cols = material.shape
    slots, edge, _ = die_power.shape
    cell = edge // RATIO
    down, across = rows // edge, cols // edge
    crows, ccols = rows // RATIO, cols // RATIO
    width = cols + LANES
    height = rows + 2 * TOP
    n_fields = 2 * layers + 1
    area = float(RATIO * RATIO)
    per = LANES // ccols
    count = grp_count * tile_count
    g = lax.axis_index("grp")
    t = lax.axis_index("tile")
    me = g * tile_count + t

    def peer(offset):
        other = lax.rem(me + offset, count)
        return other, (other // tile_count, lax.rem(other, tile_count))

    def exists(dy, dx):
        ok = jnp.bool_(True)
        if dy:
            ok = jnp.logical_and(ok, g > 0 if dy < 0 else g < grp_count - 1)
        if dx:
            ok = jnp.logical_and(ok, t > 0 if dx < 0 else t < tile_count - 1)
        return ok

    field[:, 0:TOP, :] = jnp.zeros((n_fields, TOP, width), jnp.float32)
    field[:, height - TOP : height, :] = jnp.zeros((n_fields, TOP, width), jnp.float32)
    from_side[...] = jnp.zeros_like(from_side)
    from_corner[...] = jnp.zeros_like(from_corner)
    rough_side[...] = jnp.zeros_like(rough_side)
    rough_row[...] = jnp.zeros_like(rough_row)
    rough_corner[...] = jnp.zeros_like(rough_corner)
    zx[:, 0:8, :] = jnp.zeros((layers, 8, width), jnp.float32)

    barrier = pltpu.get_barrier_semaphore()

    @pl.loop(1, count)
    def _(offset):
        pl.semaphore_signal(barrier, inc=1, device_id=peer(offset)[1], device_id_type=MESH)

    lane8 = iota((8, LANES), 1)

    @pl.loop(0, rows // 8)
    def _(i):
        r = pl.multiple_of(i * 8, 8)
        edges = jnp.zeros((8, LANES), jnp.float32)
        for f in range(n_fields):
            if f < layers:
                kind = material[f, pl.ds(r, 8), :]
                values = [jnp.full((8, cols), table[m], jnp.float32) for m in range(table.shape[0])]
                bit = 1
                while len(values) > 1:
                    odd = (kind & bit) != 0
                    values = [
                        jnp.where(odd, values[m + 1], values[m]) if m + 1 < len(values) else values[m]
                        for m in range(0, len(values), 2)
                    ]
                    bit *= 2
                x = values[0]
            elif f < 2 * layers:
                x = source[f - layers, pl.ds(r, 8), :]
            else:
                x = heat_sink[pl.ds(r, 8), :]
            field[f, pl.ds(TOP + r, 8), 0:cols] = x
            if f < layers or f == 2 * layers:
                s = f if f < layers else layers
                sums[s, pl.ds(i, 1), :] = jnp.sum(x, axis=0, keepdims=True)
            right = shift(x[:, cols - LANES :], HALO + HALO * f, 1)
            left = shift(x[:, :LANES], 64 + HALO * f, 1)
            in_right = (lane8 >= HALO * f) & (lane8 < HALO * (f + 1))
            in_left = (lane8 >= 64 + HALO * f) & (lane8 < 64 + HALO * (f + 1))
            edges = jnp.where(in_right, right, jnp.where(in_left, left, edges))
        packed[pl.ds(r, 8), :] = edges

    turned[...] = packed[...].T

    pl.semaphore_wait(barrier, count - 1)

    depth = from_side.shape[1]

    def halo_copy(k):
        dy, dx = DIRECTIONS[k]
        if dx == 0:
            src = field.at[:, pl.ds(TOP if dy < 0 else height - TOP - 8, 8), pl.ds(0, cols)]
            dst = field.at[:, pl.ds(height - TOP if dy < 0 else TOP - 8, 8), pl.ds(0, cols)]
        elif dy == 0:
            src = turned.at[pl.ds(0 if dx > 0 else 64, depth), :]
            dst = from_side.at[0 if dx > 0 else 1]
        else:
            src = packed.at[pl.ds(0 if dy < 0 else rows - 8, 8), :]
            dst = from_corner.at[k - 4]
        return pltpu.make_async_remote_copy(
            src_ref=src, dst_ref=dst, send_sem=send_sem.at[k], recv_sem=recv_sem.at[k],
            device_id=(g + dy, t + dx), device_id_type=MESH,
        )

    def rough_copy(k, phase):
        dy, dx = DIRECTIONS[k]
        half = pl.ds(2 * phase, 2)
        if dy == 0:
            src = rough.at[half]
            dst = rough_side.at[k - 2, half]
        else:
            src = rough.at[half, pl.ds(0 if dy < 0 else crows - 8, 8), :]
            dst = (rough_row.at[k, half] if dx == 0 else rough_corner.at[k - 4, half])
        s = 8 * (phase + 1) + k
        return pltpu.make_async_remote_copy(
            src_ref=src, dst_ref=dst, send_sem=send_sem.at[s], recv_sem=recv_sem.at[s],
            device_id=(g + dy, t + dx), device_id_type=MESH,
        )

    def start_all(make):
        for k, (dy, dx) in enumerate(DIRECTIONS):
            pl.when(exists(dy, dx))(lambda k=k: make(k).start())

    def wait_all_recv(make):
        for k, (dy, dx) in enumerate(DIRECTIONS):
            pl.when(exists(-dy, -dx))(lambda k=k: make(k).wait_recv())

    def wait_all_send(make):
        for k, (dy, dx) in enumerate(DIRECTIONS):
            pl.when(exists(dy, dx))(lambda k=k: make(k).wait_send())

    start_all(halo_copy)

    srow, scol = iota((edge, edge), 0), iota((edge, edge), 1)
    one, none = jnp.float32(1.0), jnp.float32(0.0)
    sides = (
        jnp.where(srow > 0, one, none) + jnp.where(srow < edge - 1, one, none)
        + jnp.where(scol > 0, one, none) + jnp.where(scol < edge - 1, one, none)
    )

    def around(v):
        return (
            jnp.where(srow > 0, shift(v, 1, 0), 0.0)
            + jnp.where(srow < edge - 1, shift(v, -1, 0), 0.0)
            + jnp.where(scol > 0, shift(v, 1, 1), 0.0)
            + jnp.where(scol < edge - 1, shift(v, -1, 1), 0.0)
        )

    rows_in = (iota((cell, edge), 0) == iota((cell, edge), 1) // RATIO).astype(jnp.float32)
    message = jnp.zeros((cell, LANES), jnp.float32)
    row_m = iota((8, LANES), 0)
    params = jnp.full((8, LANES), -1.0, jnp.float32)
    for s in range(slots):
        c, b = die_conduct[s], bond[s]
        live = jnp.where(place[s] >= 0, 1.0, 0.0)
        p = die_power[s]
        d = c * sides + b
        wt = guarded_weight(d)
        v = wt * p
        v = (1.0 - RELAX) * v + wt * (p + c * around(v))
        dies[s] = v
        resid = live * (p + c * around(v) - d * v)
        cols_in = (
            iota((edge, LANES), 0) // RATIO + cell * s == iota((edge, LANES), 1)
        ).astype(jnp.float32)
        message = message + dot(dot(rows_in, resid), cols_in)
        mine = lane8 // cell == s
        value = jnp.where(
            row_m == 0, c, jnp.where(row_m == 1, b * area, place[s].astype(jnp.float32))
        )
        params = jnp.where(mine, value, params)
    die_message[0:cell, :] = message
    die_message[cell : cell + 8, :] = params
    all_dies[me] = die_message[...]

    def gather_copy(phase, other, slot, where):
        src, dst = (die_message, all_dies) if phase == 0 else (die_fix, all_fixes)
        return pltpu.make_async_remote_copy(
            src_ref=src, dst_ref=dst.at[slot],
            send_sem=gather_send.at[phase, other], recv_sem=gather_recv.at[phase, slot],
            device_id=where, device_id_type=MESH,
        )

    def gather_start(phase):
        @pl.loop(1, count)
        def _(offset):
            other, where = peer(offset)
            gather_copy(phase, other, me, where).start()

    def gather_wait(phase):
        @pl.loop(1, count)
        def _(offset):
            other, where = peer(offset)
            gather_copy(phase, other, other, where).wait()

    gather_start(0)

    def gathered(first, total, tile):
        result = jnp.zeros((crows, LANES), jnp.float32)
        for q in range(per):
            f = tile * per + q
            if f < total:
                pick = (
                    iota((cols, LANES), 0) // RATIO + q * ccols == iota((cols, LANES), 1)
                ).astype(jnp.float32)
                result = result + dot(sums[first + f], pick)
        return result

    for tile in range(2):
        rough[tile] = gathered(0, layers + 1, tile)
    start_all(lambda k: rough_copy(k, 0))

    wait_all_recv(halo_copy)
    filler = jnp.zeros((64 - depth, rows), jnp.float32)
    arrived = jnp.concatenate([from_side[0], filler, from_side[1], filler], axis=0)
    ua[0, TOP : height - TOP, cols:width] = arrived.T
    upper = jnp.where(lane8 < 64, from_corner[3], from_corner[2])
    lower = jnp.where(lane8 < 64, from_corner[1], from_corner[0])
    ua[0, TOP - 8 : TOP, cols:width] = upper
    ua[0, height - TOP : height - TOP + 8, cols:width] = lower

    @pl.loop(1, height // 8 - 1)
    def _(i):
        r = pl.multiple_of(i * 8, 8)
        x = ua[0, pl.ds(r, 8), cols:width]
        for f in range(n_fields):
            left = shift(x, -HALO * (f + 1), 1)
            right = shift(x, -64 - HALO * f, 1)
            field[f, pl.ds(r, 8), cols:width] = jnp.where(
                lane8 >= LANES - HALO, left, jnp.where(lane8 < HALO, right, 0.0)
            )

    @pl.loop(1, height // 8 - 1)
    def _(i):
        r = pl.multiple_of(i * 8, 8)
        ks = [field[l, pl.ds(r, 8), :] for l in range(layers)]
        below = None
        for l in range(layers):
            k = ks[l]
            fx = harmonic(k, rows_at(field, l, r, 1))
            fy = harmonic(k, shift(k, -1, 1))
            zx[l, pl.ds(r, 8), :] = fx
            zy[l, pl.ds(r, 8), :] = fy
            d = fx + rows_at(zx, l, r, -1) + fy + shift(fy, 1, 1)
            if l == 0:
                d = d + field[2 * layers, pl.ds(r, 8), :]
            else:
                d = d + below
            if l < layers - 1:
                below = harmonic(k, ks[l + 1])
                zz[l, pl.ds(r, 8), :] = below
                d = d + below
            diag[l, pl.ds(r, 8), :] = d
            wt = guarded_weight(d)
            weight[l, pl.ds(r, 8), :] = wt
            ua[l, pl.ds(r, 8), :] = wt * field[layers + l, pl.ds(r, 8), :]

    def pulled(u, r, l, us):
        centre = us[l]
        fx = zx[l, pl.ds(r, 8), :]
        fy = zy[l, pl.ds(r, 8), :]
        total = field[layers + l, pl.ds(r, 8), :]
        total = total + fx * rows_at(u, l, r, 1)
        total = total + rows_at(zx, l, r, -1) * rows_at(u, l, r, -1)
        total = total + fy * shift(centre, -1, 1) + shift(fy * centre, 1, 1)
        if l > 0:
            total = total + zz[l - 1, pl.ds(r, 8), :] * us[l - 1]
        if l < layers - 1:
            total = total + zz[l, pl.ds(r, 8), :] * us[l + 1]
        return total

    def sweep(u, store, first, last):
        @pl.loop(first, last)
        def _(i):
            r = pl.multiple_of(i * 8, 8)
            us = [u[l, pl.ds(r, 8), :] for l in range(layers)]
            for l in range(layers):
                total = pulled(u, r, l, us)
                new = (1.0 - RELAX) * us[l] + weight[l, pl.ds(r, 8), :] * total
                store(l, r, new)

    def into(ref):
        def store(l, r, new):
            ref[l, pl.ds(r, 8), :] = new

        return store

    sweep(ua, into(ub), 1, height // 8 - 1)

    @pl.loop(0, crows)
    def _(i):
        r = pl.multiple_of(i * 8 + TOP, 8)
        us = [ub[l, pl.ds(r, 8), :] for l in range(layers)]
        for l in range(layers):
            resid = pulled(ub, r, l, us) - diag[l, pl.ds(r, 8), :] * us[l]
            sums[layers + 1 + l, pl.ds(i, 1), :] = jnp.sum(resid[:, :cols], axis=0, keepdims=True)

    for tile in range(2):
        rough[2 + tile] = gathered(layers + 1, layers, tile)
    start_all(lambda k: rough_copy(k, 1))

    gather_wait(0)
    span = tile_count * across
    chigh = crows + 16
    parts = cell + 8
    spots = [(a, b) for a in range(-1, down + 1) for b in range(-1, across + 1)]
    wanted = []
    for a, b in spots:
        pr, pc = g * down + a, t * across + b
        inside = (pr >= 0) & (pr < grp_count * down) & (pc >= 0) & (pc < span)
        wanted.append(jnp.where(inside, pr * span + pc, -2).astype(jnp.float32))

    for lo in range(0, len(spots), across + 2):

        def add(d, acc, lo=lo):
            block = all_dies[d]
            where = block[cell + 2 : cell + 3, :]
            return tuple(
                a + jnp.where(where == wanted[lo + j], block, 0.0) for j, a in enumerate(acc)
            )

        acc = lax.fori_loop(
            0, count, add, tuple(jnp.zeros((parts, LANES), jnp.float32) for _ in range(across + 2))
        )
        lane_p = iota((parts, LANES), 1)
        line = jnp.zeros((parts, LANES), jnp.float32)
        for j in range(across + 2):
            x = acc[j]
            step = LANES // 2
            while step >= cell:
                x = x + shift(x, step, 1)
                step //= 2
            line = jnp.where(lane_p // cell == j, x, line)
        line = shift(line, 8 - cell, 1)
        a = lo // (across + 2) - 1
        if a == -1:
            first, size, off = 0, 8, cell - 8
        elif a == down:
            first, size, off = 8 + crows, 8, 0
        else:
            first, size, off = 8 + a * cell, cell, 0
        n = 2 * layers + 1
        wide[n, first : first + size, :] = line[off : off + size]
        wide[n + 1, first : first + size, :] = jnp.broadcast_to(
            line[cell : cell + 1], (size, LANES)
        )
        wide[n + 2, first : first + size, :] = jnp.broadcast_to(
            line[cell + 1 : cell + 2], (size, LANES)
        )

    for phase in range(2):
        wait_all_recv(lambda k: rough_copy(k, phase))
        for f in range(layers + 1 if phase == 0 else layers):
            tile, q = 2 * phase + f // per, f % per
            target = f if phase == 0 else layers + 1 + f

            def joined(left, middle, right, size):
                lane = iota((size, LANES), 1)
                x = shift(middle, 8 - ccols * q, 1)
                x = jnp.where((lane >= 8) & (lane < 8 + ccols), x, 0.0)
                x = jnp.where(lane < 8, shift(left, 8 - ccols - ccols * q, 1), x)
                return jnp.where(
                    (lane >= 8 + ccols) & (lane < 16 + ccols),
                    shift(right, 8 + ccols - ccols * q, 1),
                    x,
                )

            wide[target, 8 : 8 + crows, :] = joined(
                rough_side[1, tile], rough[tile], rough_side[0, tile], crows
            )
            wide[target, 0:8, :] = joined(
                rough_corner[3, tile], rough_row[1, tile], rough_corner[2, tile], 8
            )
            wide[target, 8 + crows : chigh, :] = joined(
                rough_corner[1, tile], rough_row[0, tile], rough_corner[0, tile], 8
            )

    kc = [wide[l] * (1.0 / area) for l in range(layers)]
    cx = [harmonic(k, shift(k, -1, 0)) for k in kc]
    cy = [harmonic(k, shift(k, -1, 1)) for k in kc]
    cz = [harmonic(kc[l], kc[l + 1]) * area for l in range(layers - 1)]
    top_rhs, top_c, top_b = (wide[2 * layers + 1 + j] for j in range(3))
    weights = []
    for l in range(layers):
        d = cx[l] + shift(cx[l], 1, 0) + cy[l] + shift(cy[l], 1, 1)
        if l == 0:
            d = d + wide[layers]
        else:
            d = d + cz[l - 1]
        d = d + (cz[l] if l < layers - 1 else top_b)
        weights.append(guarded_weight(d))
    crow = (iota((chigh, LANES), 0) + (cell - 8)) % cell
    ccol = (iota((chigh, LANES), 1) + (cell - 8)) % cell
    low_x, high_x = crow != 0, crow != cell - 1
    low_y, high_y = ccol != 0, ccol != cell - 1
    near = sum(jnp.where(m, one, none) for m in (low_x, high_x, low_y, high_y))
    top_d = top_c * near + top_b
    top_w = guarded_weight(top_d)
    errors = [weights[l] * wide[layers + 1 + l] for l in range(layers)]
    top = top_w * top_rhs
    for _ in range(NC - 1):
        new = []
        for l in range(layers):
            e = errors[l]
            total = wide[layers + 1 + l]
            total = total + cx[l] * shift(e, -1, 0) + shift(cx[l] * e, 1, 0)
            total = total + cy[l] * shift(e, -1, 1) + shift(cy[l] * e, 1, 1)
            if l > 0:
                total = total + cz[l - 1] * errors[l - 1]
            total = total + (cz[l] * errors[l + 1] if l < layers - 1 else top_b * top)
            new.append((1.0 - RELAX) * e + weights[l] * total)
        nearby = (
            jnp.where(low_x, shift(top, 1, 0), 0.0)
            + jnp.where(high_x, shift(top, -1, 0), 0.0)
            + jnp.where(low_y, shift(top, 1, 1), 0.0)
            + jnp.where(high_y, shift(top, -1, 1), 0.0)
        )
        top = top + top_w * (
            top_rhs + top_b * errors[layers - 1] + top_c * nearby - top_d * top
        )
        errors = new
    for l in range(layers):
        solved[l] = errors[l]

    lane_c = iota((cell, LANES), 1)
    fix = jnp.zeros((cell, LANES), jnp.float32)
    for a in range(down):
        piece = shift(top[8 + a * cell : 8 + (a + 1) * cell], a * ccols - 8, 1)
        fix = jnp.where(lane_c // ccols == a, piece, fix)
    die_fix[...] = fix
    all_fixes[me] = die_fix[...]
    gather_start(1)

    column = iota((LANES, width), 1)
    source_lane = jnp.where(column < cols + LANES // 2, 8 + column // RATIO, 7)
    pick = (iota((LANES, width), 0) == source_lane).astype(jnp.float32)
    for l in range(layers):
        spread[l] = dot(solved[l], pick)

    @pl.loop(1, height // 8 - 1)
    def _(i):
        r = pl.multiple_of(i * 8, 8)
        for l in range(layers):
            ub[l, pl.ds(r, 8), :] = ub[l, pl.ds(r, 8), :] + spread[l, pl.ds(i + 6, 1), :]

    sweep(ub, into(ua), 1, height // 8 - 1)

    def finish(l, r, new):
        out[l, pl.ds(r - TOP, 8), :] = new[:, :cols]

    sweep(ua, finish, TOP // 8, (height - TOP) // 8)

    gather_wait(1)
    codes = []
    for s in range(slots):
        spot = jnp.maximum(place[s], 0)
        pr, pc = spot // span, lax.rem(spot, span)
        target = (pr // down) * tile_count + pc // across
        local = lax.rem(pr, down) * across + lax.rem(pc, across)
        codes.append(jnp.where(place[s] >= 0, target * 8 + local, -1))
    group = lane_c // cell

    def collect(d, acc):
        block = all_fixes[d]
        code = group + d * 8
        return tuple(a + jnp.where(code == codes[s], block, 0.0) for s, a in enumerate(acc))

    fixes = lax.fori_loop(
        0, count, collect, tuple(jnp.zeros((cell, LANES), jnp.float32) for _ in range(slots))
    )
    rows_out = (iota((edge, cell), 0) // RATIO == iota((edge, cell), 1)).astype(jnp.float32)
    cols_out = (iota((LANES, edge), 0) == iota((LANES, edge), 1) // RATIO).astype(jnp.float32)
    for s in range(slots):
        x = fixes[s]
        step = LANES // 2
        while step >= cell:
            x = x + shift(x, step, 1)
            step //= 2
        c, b = die_conduct[s], bond[s]
        live = jnp.where(place[s] >= 0, 1.0, 0.0)
        p = die_power[s]
        wt = guarded_weight(c * sides + b)
        v = dies[s] + live * dot(rows_out, dot(x, cols_out))
        for _ in range(NU):
            v = (1.0 - RELAX) * v + wt * (p + c * around(v))
        die_out[s] = live * v

    wait_all_send(halo_copy)
    for phase in range(2):
        wait_all_send(lambda k: rough_copy(k, phase))


def per_device(grp_count, tile_count, *args):
    material, die_power = args[0], args[4]
    layers, rows, cols = material.shape
    slots, edge, _ = die_power.shape
    cell = edge // RATIO
    crows = rows // RATIO
    width, height = cols + LANES, rows + 2 * TOP
    count = grp_count * tile_count
    n_fields = 2 * layers + 1
    depth = -(-n_fields * HALO // 8) * 8
    vmem = pl.BlockSpec(memory_space=pltpu.VMEM)
    smem = pl.BlockSpec(memory_space=pltpu.SMEM)
    f32 = jnp.float32

    def scratch(*shape):
        return pltpu.VMEM(shape, f32)

    grid = (layers, height, width)
    return pl.pallas_call(
        functools.partial(kernel, grp_count, tile_count),
        out_shape=(
            jax.ShapeDtypeStruct((layers, rows, cols), f32),
            jax.ShapeDtypeStruct((slots, edge, edge), f32),
        ),
        in_specs=[vmem, smem, vmem, vmem, vmem, smem, smem, smem],
        out_specs=(vmem, vmem),
        scratch_shapes=[
            scratch(n_fields, height, width),
            scratch(*grid),
            scratch(*grid),
            scratch(layers - 1, height, width),
            scratch(*grid),
            scratch(*grid),
            scratch(*grid),
            scratch(*grid),
            scratch(rows, LANES),
            scratch(LANES, rows),
            scratch(2, depth, rows),
            scratch(4, 8, LANES),
            scratch(n_fields, crows, cols),
            scratch(4, crows, LANES),
            scratch(2, 4, crows, LANES),
            scratch(2, 4, 8, LANES),
            scratch(4, 4, 8, LANES),
            scratch(slots, edge, edge),
            scratch(cell + 8, LANES),
            scratch(count, cell + 8, LANES),
            scratch(cell, LANES),
            scratch(count, cell, LANES),
            scratch(n_fields + 3, crows + 16, LANES),
            scratch(layers, crows + 16, LANES),
            scratch(layers, crows + 16, width),
            pltpu.SemaphoreType.DMA((24,)),
            pltpu.SemaphoreType.DMA((24,)),
            pltpu.SemaphoreType.DMA((2, count)),
            pltpu.SemaphoreType.DMA((2, count)),
        ],
        compiler_params=pltpu.CompilerParams(
            collective_id=0, has_side_effects=True, vmem_limit_bytes=60 * 1024 * 1024
        ),
    )(*args)


def solution(mesh):
    placed = (
        P(None, "grp", "tile"),
        P(),
        P("grp", "tile"),
        P(None, "grp", "tile"),
        P(("grp", "tile"), None, None),
        P(("grp", "tile")),
        P(("grp", "tile")),
        P(("grp", "tile")),
    )
    return jax.shard_map(
        functools.partial(per_device, mesh.shape["grp"], mesh.shape["tile"]),
        mesh=mesh,
        in_specs=placed,
        out_specs=(P(None, "grp", "tile"), P(("grp", "tile"), None, None)),
        check_vma=False,
    )
```

```python
import functools
import jax
import jax.numpy as jnp
from jax import lax
from jax.experimental import pallas as pl
from jax.experimental.pallas import tpu as pltpu
from jax.sharding import PartitionSpec as P

RATIO = 8
NU = 2
NC = 4
RELAX = 0.8
HALO = 4
TOP = 16
LANES = 128
MESH = pl.DeviceIdType.MESH
HIGHEST = lax.Precision.HIGHEST
DIRECTIONS = ((-1, 0), (1, 0), (0, -1), (0, 1), (-1, -1), (-1, 1), (1, -1), (1, 1))


def inverse(x):
    r = pl.reciprocal(x, approx=True)
    return r * (2.0 - x * r)


def harmonic(a, b):
    total = a + b
    return 2.0 * a * b * inverse(jnp.where(total > 0, total, 1.0))


def guarded_weight(d):
    return RELAX * inverse(jnp.where(d > 0, d, 1.0))


def iota(shape, dim):
    return lax.broadcasted_iota(jnp.int32, shape, dim)


def shift(x, amount, axis):
    return pltpu.roll(x, amount % x.shape[axis], axis)


def rows_at(ref, l, r, offset):
    if offset < 0:
        return ref.at[l, pl.ds(pl.multiple_of(r - 8, 8), 16), :][8 + offset : 16 + offset, :]
    return ref.at[l, pl.ds(r, 16), :][offset : 8 + offset, :]


def row_sums(fields):
    shape = fields[0].shape
    row = lax.broadcasted_iota(jnp.int32, shape, 0)
    xs = list(fields) + [jnp.zeros(shape, jnp.float32)] * (8 - len(fields))

    def merge(x, y, start, run):
        first = ((row - start + 8) % 8) % (2 * run) < run
        return jnp.where(first, x, y) + shift(jnp.where(first, y, x), -run, 0)

    z = [merge(xs[j], xs[j + 4], j, 4) for j in range(4)]
    y = [merge(z[j], z[j + 2], j, 2) for j in range(2)]
    return merge(y[0], y[1], 0, 1)


def dot(a, b):
    return jnp.dot(a, b, precision=HIGHEST, preferred_element_type=jnp.float32)


def kernel(
    grp_count,
    tile_count,
    material,
    table,
    heat_sink,
    source,
    die_power,
    die_conduct,
    bond,
    place,
    out,
    die_out,
    field,
    zx,
    zy,
    zz,
    diag,
    weight,
    ua,
    ub,
    packed,
    turned,
    from_side,
    from_corner,
    sums,
    folded,
    arrived,
    rough,
    rough_side,
    rough_row,
    rough_corner,
    dies,
    die_message,
    all_dies,
    die_fix,
    all_fixes,
    wide,
    solved,
    spread,
    send_sem,
    recv_sem,
    gather_send,
    gather_recv,
):
    layers, rows, cols = material.shape
    slots, edge, _ = die_power.shape
    cell = edge // RATIO
    down, across = rows // edge, cols // edge
    crows, ccols = rows // RATIO, cols // RATIO
    width = cols + LANES
    height = rows + 2 * TOP
    n_fields = 2 * layers + 1
    area = float(RATIO * RATIO)
    per = LANES // ccols
    count = grp_count * tile_count
    g = lax.axis_index("grp")
    t = lax.axis_index("tile")
    me = g * tile_count + t

    def peer(offset):
        other = lax.rem(me + offset, count)
        return other, (other // tile_count, lax.rem(other, tile_count))

    def exists(dy, dx):
        ok = jnp.bool_(True)
        if dy:
            ok = jnp.logical_and(ok, g > 0 if dy < 0 else g < grp_count - 1)
        if dx:
            ok = jnp.logical_and(ok, t > 0 if dx < 0 else t < tile_count - 1)
        return ok

    field[:, 0:TOP, :] = jnp.zeros((n_fields, TOP, width), jnp.float32)
    field[:, height - TOP : height, :] = jnp.zeros((n_fields, TOP, width), jnp.float32)
    from_side[...] = jnp.zeros_like(from_side)
    from_corner[...] = jnp.zeros_like(from_corner)
    rough_side[...] = jnp.zeros_like(rough_side)
    rough_row[...] = jnp.zeros_like(rough_row)
    rough_corner[...] = jnp.zeros_like(rough_corner)
    zx[:, 0:8, :] = jnp.zeros((layers, 8, width), jnp.float32)

    barrier = pltpu.get_barrier_semaphore()

    @pl.loop(1, count)
    def _(offset):
        pl.semaphore_signal(barrier, inc=1, device_id=peer(offset)[1], device_id_type=MESH)

    lane8 = iota((8, LANES), 1)

    @pl.loop(0, rows // 8)
    def _(i):
        r = pl.multiple_of(i * 8, 8)
        edges = jnp.zeros((8, LANES), jnp.float32)
        summed = []
        for f in range(n_fields):
            if f < layers:
                kind = material[f, pl.ds(r, 8), :]
                values = [jnp.full((8, cols), table[m], jnp.float32) for m in range(table.shape[0])]
                bit = 1
                while len(values) > 1:
                    odd = (kind & bit) != 0
                    values = [
                        jnp.where(odd, values[m + 1], values[m]) if m + 1 < len(values) else values[m]
                        for m in range(0, len(values), 2)
                    ]
                    bit *= 2
                x = values[0]
            elif f < 2 * layers:
                x = source[f - layers, pl.ds(r, 8), :]
            else:
                x = heat_sink[pl.ds(r, 8), :]
            field[f, pl.ds(TOP + r, 8), 0:cols] = x
            if f < layers or f == 2 * layers:
                summed.append(x)
            right = shift(x[:, cols - LANES :], HALO + HALO * f, 1)
            left = shift(x[:, :LANES], 64 + HALO * f, 1)
            in_right = (lane8 >= HALO * f) & (lane8 < HALO * (f + 1))
            in_left = (lane8 >= 64 + HALO * f) & (lane8 < 64 + HALO * (f + 1))
            edges = jnp.where(in_right, right, jnp.where(in_left, left, edges))
        packed[pl.ds(r, 8), :] = edges
        sums[pl.ds(r, 8), :] = row_sums(summed)

    turned[...] = packed[...].T

    pl.semaphore_wait(barrier, count - 1)

    depth = from_side.shape[1]

    def halo_copy(k):
        dy, dx = DIRECTIONS[k]
        if dx == 0:
            src = field.at[:, pl.ds(TOP if dy < 0 else height - TOP - 8, 8), pl.ds(0, cols)]
            dst = field.at[:, pl.ds(height - TOP if dy < 0 else TOP - 8, 8), pl.ds(0, cols)]
        elif dy == 0:
            src = turned.at[pl.ds(0 if dx > 0 else 64, depth), :]
            dst = from_side.at[0 if dx > 0 else 1]
        else:
            src = packed.at[pl.ds(0 if dy < 0 else rows - 8, 8), :]
            dst = from_corner.at[k - 4]
        return pltpu.make_async_remote_copy(
            src_ref=src, dst_ref=dst, send_sem=send_sem.at[k], recv_sem=recv_sem.at[k],
            device_id=(g + dy, t + dx), device_id_type=MESH,
        )

    def rough_copy(k, phase):
        dy, dx = DIRECTIONS[k]
        half = pl.ds(2 * phase, 2)
        if dy == 0:
            src = rough.at[half]
            dst = rough_side.at[k - 2, half]
        else:
            src = rough.at[half, pl.ds(0 if dy < 0 else crows - 8, 8), :]
            dst = (rough_row.at[k, half] if dx == 0 else rough_corner.at[k - 4, half])
        s = 8 * (phase + 1) + k
        return pltpu.make_async_remote_copy(
            src_ref=src, dst_ref=dst, send_sem=send_sem.at[s], recv_sem=recv_sem.at[s],
            device_id=(g + dy, t + dx), device_id_type=MESH,
        )

    def start_all(make):
        for k, (dy, dx) in enumerate(DIRECTIONS):
            pl.when(exists(dy, dx))(lambda k=k: make(k).start())

    def wait_all_recv(make):
        for k, (dy, dx) in enumerate(DIRECTIONS):
            pl.when(exists(-dy, -dx))(lambda k=k: make(k).wait_recv())

    def wait_all_send(make):
        for k, (dy, dx) in enumerate(DIRECTIONS):
            pl.when(exists(dy, dx))(lambda k=k: make(k).wait_send())

    start_all(halo_copy)

    srow, scol = iota((edge, edge), 0), iota((edge, edge), 1)
    one, none = jnp.float32(1.0), jnp.float32(0.0)
    sides = (
        jnp.where(srow > 0, one, none) + jnp.where(srow < edge - 1, one, none)
        + jnp.where(scol > 0, one, none) + jnp.where(scol < edge - 1, one, none)
    )

    def around(v):
        return (
            jnp.where(srow > 0, shift(v, 1, 0), 0.0)
            + jnp.where(srow < edge - 1, shift(v, -1, 0), 0.0)
            + jnp.where(scol > 0, shift(v, 1, 1), 0.0)
            + jnp.where(scol < edge - 1, shift(v, -1, 1), 0.0)
        )

    rows_in = (iota((cell, edge), 0) == iota((cell, edge), 1) // RATIO).astype(jnp.float32)
    message = jnp.zeros((cell, LANES), jnp.float32)
    row_m = iota((8, LANES), 0)
    params = jnp.full((8, LANES), -1.0, jnp.float32)
    for s in range(slots):
        c, b = die_conduct[s], bond[s]
        live = jnp.where(place[s] >= 0, 1.0, 0.0)
        p = die_power[s]
        d = c * sides + b
        wt = guarded_weight(d)
        v = wt * p
        v = (1.0 - RELAX) * v + wt * (p + c * around(v))
        dies[s] = v
        resid = live * (p + c * around(v) - d * v)
        cols_in = (
            iota((edge, LANES), 0) // RATIO + cell * s == iota((edge, LANES), 1)
        ).astype(jnp.float32)
        message = message + dot(dot(rows_in, resid), cols_in)
        mine = lane8 // cell == s
        value = jnp.where(
            row_m == 0, c, jnp.where(row_m == 1, b * area, place[s].astype(jnp.float32))
        )
        params = jnp.where(mine, value, params)
    die_message[0:cell, :] = message
    die_message[cell : cell + 8, :] = params
    all_dies[me] = die_message[...]

    def gather_copy(phase, other, slot, where):
        src, dst = (die_message, all_dies) if phase == 0 else (die_fix, all_fixes)
        return pltpu.make_async_remote_copy(
            src_ref=src, dst_ref=dst.at[slot],
            send_sem=gather_send.at[phase, other], recv_sem=gather_recv.at[phase, slot],
            device_id=where, device_id_type=MESH,
        )

    def gather_start(phase):
        @pl.loop(1, count)
        def _(offset):
            other, where = peer(offset)
            gather_copy(phase, other, me, where).start()

    def gather_wait(phase):
        @pl.loop(1, count)
        def _(offset):
            other, where = peer(offset)
            gather_copy(phase, other, other, where).wait()

    gather_start(0)

    def gathered(total, first_tile):
        pick = (iota((cols, LANES), 0) // RATIO == iota((cols, LANES), 1)).astype(jnp.float32)
        folded[...] = dot(sums[...], pick)
        for tile in range(2):
            result = jnp.zeros((crows, LANES), jnp.float32)
            for q in range(per):
                f = tile * per + q
                if f < total:
                    result = result + shift(folded[pl.ds(f, crows, stride=8), :], q * ccols, 1)
            rough[first_tile + tile] = result

    gathered(layers + 1, 0)
    start_all(lambda k: rough_copy(k, 0))

    wait_all_recv(halo_copy)
    pairs = []
    for f in range(n_fields):
        pairs.append(from_side[0, HALO * f : HALO * (f + 1), :])
        pairs.append(from_side[1, HALO * f : HALO * (f + 1), :])
    pairs.append(jnp.zeros((LANES - 2 * HALO * n_fields, rows), jnp.float32))
    arrived[TOP : height - TOP, :] = jnp.concatenate(pairs, axis=0).T

    def corner(x, y):
        tile = jnp.zeros((8, LANES), jnp.float32)
        for f in range(n_fields):
            at = lane8 - 2 * HALO * f
            tile = jnp.where((at >= 0) & (at < HALO), shift(x, HALO * f, 1), tile)
            tile = jnp.where(
                (at >= HALO) & (at < 2 * HALO), shift(y, HALO * f + HALO - 64, 1), tile
            )
        return tile

    arrived[0 : TOP - 8, :] = jnp.zeros((TOP - 8, LANES), jnp.float32)
    arrived[TOP - 8 : TOP, :] = corner(from_corner[3], from_corner[2])
    arrived[height - TOP : height - TOP + 8, :] = corner(from_corner[1], from_corner[0])
    arrived[height - TOP + 8 : height, :] = jnp.zeros((TOP - 8, LANES), jnp.float32)
    in_halo = (lane8 < HALO) | (lane8 >= LANES - HALO)

    def unpack(r):
        x = arrived[pl.ds(r, 8), :]
        for f in range(n_fields):
            field[f, pl.ds(r, 8), cols:width] = jnp.where(
                in_halo, shift(x, -HALO * (2 * f + 1), 1), 0.0
            )

    unpack(8)

    @pl.loop(1, height // 8 - 1)
    def _(i):
        r = pl.multiple_of(i * 8, 8)
        unpack(pl.multiple_of(r + 8, 8))
        ks = [field[l, pl.ds(r, 8), :] for l in range(layers)]
        below = None
        for l in range(layers):
            k = ks[l]
            fx = harmonic(k, rows_at(field, l, r, 1))
            fy = harmonic(k, shift(k, -1, 1))
            zx[l, pl.ds(r, 8), :] = fx
            zy[l, pl.ds(r, 8), :] = fy
            d = fx + rows_at(zx, l, r, -1) + fy + shift(fy, 1, 1)
            if l == 0:
                d = d + field[2 * layers, pl.ds(r, 8), :]
            else:
                d = d + below
            if l < layers - 1:
                below = harmonic(k, ks[l + 1])
                zz[l, pl.ds(r, 8), :] = below
                d = d + below
            diag[l, pl.ds(r, 8), :] = d
            wt = guarded_weight(d)
            weight[l, pl.ds(r, 8), :] = wt
            ua[l, pl.ds(r, 8), :] = wt * field[layers + l, pl.ds(r, 8), :]

    def pulled(u, r, l, us):
        centre = us[l]
        fx = zx[l, pl.ds(r, 8), :]
        fy = zy[l, pl.ds(r, 8), :]
        total = field[layers + l, pl.ds(r, 8), :]
        total = total + fx * rows_at(u, l, r, 1)
        total = total + rows_at(zx, l, r, -1) * rows_at(u, l, r, -1)
        total = total + fy * shift(centre, -1, 1) + shift(fy * centre, 1, 1)
        if l > 0:
            total = total + zz[l - 1, pl.ds(r, 8), :] * us[l - 1]
        if l < layers - 1:
            total = total + zz[l, pl.ds(r, 8), :] * us[l + 1]
        return total

    def sweep(u, store, first, last):
        @pl.loop(first, last)
        def _(i):
            r = pl.multiple_of(i * 8, 8)
            us = [u[l, pl.ds(r, 8), :] for l in range(layers)]
            for l in range(layers):
                total = pulled(u, r, l, us)
                new = (1.0 - RELAX) * us[l] + weight[l, pl.ds(r, 8), :] * total
                store(l, r, new)

    def into(ref):
        def store(l, r, new):
            ref[l, pl.ds(r, 8), :] = new

        return store

    sweep(ua, into(ub), 1, height // 8 - 1)

    @pl.loop(0, crows)
    def _(i):
        r = pl.multiple_of(i * 8 + TOP, 8)
        us = [ub[l, pl.ds(r, 8), :] for l in range(layers)]
        resids = []
        for l in range(layers):
            resid = pulled(ub, r, l, us) - diag[l, pl.ds(r, 8), :] * us[l]
            resids.append(resid[:, :cols])
        sums[pl.ds(pl.multiple_of(i * 8, 8), 8), :] = row_sums(resids)

    gathered(layers, 2)
    start_all(lambda k: rough_copy(k, 1))

    gather_wait(0)
    span = tile_count * across
    chigh = crows + 16
    parts = cell + 8
    spots = [(a, b) for a in range(-1, down + 1) for b in range(-1, across + 1)]
    wanted = []
    for a, b in spots:
        pr, pc = g * down + a, t * across + b
        inside = (pr >= 0) & (pr < grp_count * down) & (pc >= 0) & (pc < span)
        wanted.append(jnp.where(inside, pr * span + pc, -2).astype(jnp.float32))

    for lo in range(0, len(spots), across + 2):

        def add(d, acc, lo=lo):
            block = all_dies[d]
            where = block[cell + 2 : cell + 3, :]
            return tuple(
                a + jnp.where(where == wanted[lo + j], block, 0.0) for j, a in enumerate(acc)
            )

        acc = lax.fori_loop(
            0, count, add, tuple(jnp.zeros((parts, LANES), jnp.float32) for _ in range(across + 2))
        )
        lane_p = iota((parts, LANES), 1)
        line = jnp.zeros((parts, LANES), jnp.float32)
        for j in range(across + 2):
            x = acc[j]
            step = LANES // 2
            while step >= cell:
                x = x + shift(x, step, 1)
                step //= 2
            line = jnp.where(lane_p // cell == j, x, line)
        line = shift(line, 8 - cell, 1)
        a = lo // (across + 2) - 1
        if a == -1:
            first, size, off = 0, 8, cell - 8
        elif a == down:
            first, size, off = 8 + crows, 8, 0
        else:
            first, size, off = 8 + a * cell, cell, 0
        n = 2 * layers + 1
        wide[n, first : first + size, :] = line[off : off + size]
        wide[n + 1, first : first + size, :] = jnp.broadcast_to(
            line[cell : cell + 1], (size, LANES)
        )
        wide[n + 2, first : first + size, :] = jnp.broadcast_to(
            line[cell + 1 : cell + 2], (size, LANES)
        )

    for phase in range(2):
        wait_all_recv(lambda k: rough_copy(k, phase))
        for f in range(layers + 1 if phase == 0 else layers):
            tile, q = 2 * phase + f // per, f % per
            target = f if phase == 0 else layers + 1 + f

            def joined(left, middle, right, size):
                lane = iota((size, LANES), 1)
                x = shift(middle, 8 - ccols * q, 1)
                x = jnp.where((lane >= 8) & (lane < 8 + ccols), x, 0.0)
                x = jnp.where(lane < 8, shift(left, 8 - ccols - ccols * q, 1), x)
                return jnp.where(
                    (lane >= 8 + ccols) & (lane < 16 + ccols),
                    shift(right, 8 + ccols - ccols * q, 1),
                    x,
                )

            wide[target, 8 : 8 + crows, :] = joined(
                rough_side[1, tile], rough[tile], rough_side[0, tile], crows
            )
            wide[target, 0:8, :] = joined(
                rough_corner[3, tile], rough_row[1, tile], rough_corner[2, tile], 8
            )
            wide[target, 8 + crows : chigh, :] = joined(
                rough_corner[1, tile], rough_row[0, tile], rough_corner[0, tile], 8
            )

    kc = [wide[l] * (1.0 / area) for l in range(layers)]
    cx = [harmonic(k, shift(k, -1, 0)) for k in kc]
    cy = [harmonic(k, shift(k, -1, 1)) for k in kc]
    cz = [harmonic(kc[l], kc[l + 1]) * area for l in range(layers - 1)]
    top_rhs, top_c, top_b = (wide[2 * layers + 1 + j] for j in range(3))
    weights = []
    for l in range(layers):
        d = cx[l] + shift(cx[l], 1, 0) + cy[l] + shift(cy[l], 1, 1)
        if l == 0:
            d = d + wide[layers]
        else:
            d = d + cz[l - 1]
        d = d + (cz[l] if l < layers - 1 else top_b)
        weights.append(guarded_weight(d))
    crow = (iota((chigh, LANES), 0) + (cell - 8)) % cell
    ccol = (iota((chigh, LANES), 1) + (cell - 8)) % cell
    low_x, high_x = crow != 0, crow != cell - 1
    low_y, high_y = ccol != 0, ccol != cell - 1
    near = sum(jnp.where(m, one, none) for m in (low_x, high_x, low_y, high_y))
    top_d = top_c * near + top_b
    top_w = guarded_weight(top_d)
    errors = [weights[l] * wide[layers + 1 + l] for l in range(layers)]
    top = top_w * top_rhs
    for _ in range(NC - 1):
        new = []
        for l in range(layers):
            e = errors[l]
            total = wide[layers + 1 + l]
            total = total + cx[l] * shift(e, -1, 0) + shift(cx[l] * e, 1, 0)
            total = total + cy[l] * shift(e, -1, 1) + shift(cy[l] * e, 1, 1)
            if l > 0:
                total = total + cz[l - 1] * errors[l - 1]
            total = total + (cz[l] * errors[l + 1] if l < layers - 1 else top_b * top)
            new.append((1.0 - RELAX) * e + weights[l] * total)
        nearby = (
            jnp.where(low_x, shift(top, 1, 0), 0.0)
            + jnp.where(high_x, shift(top, -1, 0), 0.0)
            + jnp.where(low_y, shift(top, 1, 1), 0.0)
            + jnp.where(high_y, shift(top, -1, 1), 0.0)
        )
        top = top + top_w * (
            top_rhs + top_b * errors[layers - 1] + top_c * nearby - top_d * top
        )
        errors = new
    for l in range(layers):
        solved[l] = errors[l]

    lane_c = iota((cell, LANES), 1)
    fix = jnp.zeros((cell, LANES), jnp.float32)
    for a in range(down):
        piece = shift(top[8 + a * cell : 8 + (a + 1) * cell], a * ccols - 8, 1)
        fix = jnp.where(lane_c // ccols == a, piece, fix)
    die_fix[...] = fix
    all_fixes[me] = die_fix[...]
    gather_start(1)

    column = iota((LANES, width), 1)
    source_lane = jnp.where(column < cols + LANES // 2, 8 + column // RATIO, 7)
    pick = (iota((LANES, width), 0) == source_lane).astype(jnp.float32)
    for l in range(layers):
        spread[l] = dot(solved[l], pick)

    @pl.loop(1, height // 8 - 1)
    def _(i):
        r = pl.multiple_of(i * 8, 8)
        for l in range(layers):
            ub[l, pl.ds(r, 8), :] = ub[l, pl.ds(r, 8), :] + spread[l, pl.ds(i + 6, 1), :]

    sweep(ub, into(ua), 1, height // 8 - 1)

    def finish(l, r, new):
        out[l, pl.ds(r - TOP, 8), :] = new[:, :cols]

    sweep(ua, finish, TOP // 8, (height - TOP) // 8)

    gather_wait(1)
    codes = []
    for s in range(slots):
        spot = jnp.maximum(place[s], 0)
        pr, pc = spot // span, lax.rem(spot, span)
        target = (pr // down) * tile_count + pc // across
        local = lax.rem(pr, down) * across + lax.rem(pc, across)
        codes.append(jnp.where(place[s] >= 0, target * 8 + local, -1))
    group = lane_c // cell

    def collect(d, acc):
        block = all_fixes[d]
        code = group + d * 8
        return tuple(a + jnp.where(code == codes[s], block, 0.0) for s, a in enumerate(acc))

    fixes = lax.fori_loop(
        0, count, collect, tuple(jnp.zeros((cell, LANES), jnp.float32) for _ in range(slots))
    )
    rows_out = (iota((edge, cell), 0) // RATIO == iota((edge, cell), 1)).astype(jnp.float32)
    cols_out = (iota((LANES, edge), 0) == iota((LANES, edge), 1) // RATIO).astype(jnp.float32)
    for s in range(slots):
        x = fixes[s]
        step = LANES // 2
        while step >= cell:
            x = x + shift(x, step, 1)
            step //= 2
        c, b = die_conduct[s], bond[s]
        live = jnp.where(place[s] >= 0, 1.0, 0.0)
        p = die_power[s]
        wt = guarded_weight(c * sides + b)
        v = dies[s] + live * dot(rows_out, dot(x, cols_out))
        for _ in range(NU):
            v = (1.0 - RELAX) * v + wt * (p + c * around(v))
        die_out[s] = live * v

    wait_all_send(halo_copy)
    for phase in range(2):
        wait_all_send(lambda k: rough_copy(k, phase))


def per_device(grp_count, tile_count, *args):
    material, die_power = args[0], args[4]
    layers, rows, cols = material.shape
    slots, edge, _ = die_power.shape
    cell = edge // RATIO
    crows = rows // RATIO
    width, height = cols + LANES, rows + 2 * TOP
    count = grp_count * tile_count
    n_fields = 2 * layers + 1
    depth = -(-n_fields * HALO // 8) * 8
    vmem = pl.BlockSpec(memory_space=pltpu.VMEM)
    smem = pl.BlockSpec(memory_space=pltpu.SMEM)
    f32 = jnp.float32

    def scratch(*shape):
        return pltpu.VMEM(shape, f32)

    grid = (layers, height, width)
    return pl.pallas_call(
        functools.partial(kernel, grp_count, tile_count),
        out_shape=(
            jax.ShapeDtypeStruct((layers, rows, cols), f32),
            jax.ShapeDtypeStruct((slots, edge, edge), f32),
        ),
        in_specs=[vmem, smem, vmem, vmem, vmem, smem, smem, smem],
        out_specs=(vmem, vmem),
        scratch_shapes=[
            scratch(n_fields, height, width),
            scratch(*grid),
            scratch(*grid),
            scratch(layers - 1, height, width),
            scratch(*grid),
            scratch(*grid),
            scratch(*grid),
            scratch(*grid),
            scratch(rows, LANES),
            scratch(LANES, rows),
            scratch(2, depth, rows),
            scratch(4, 8, LANES),
            scratch(rows, cols),
            scratch(rows, LANES),
            scratch(height, LANES),
            scratch(4, crows, LANES),
            scratch(2, 4, crows, LANES),
            scratch(2, 4, 8, LANES),
            scratch(4, 4, 8, LANES),
            scratch(slots, edge, edge),
            scratch(cell + 8, LANES),
            scratch(count, cell + 8, LANES),
            scratch(cell, LANES),
            scratch(count, cell, LANES),
            scratch(n_fields + 3, crows + 16, LANES),
            scratch(layers, crows + 16, LANES),
            scratch(layers, crows + 16, width),
            pltpu.SemaphoreType.DMA((24,)),
            pltpu.SemaphoreType.DMA((24,)),
            pltpu.SemaphoreType.DMA((2, count)),
            pltpu.SemaphoreType.DMA((2, count)),
        ],
        compiler_params=pltpu.CompilerParams(
            collective_id=0, has_side_effects=True, vmem_limit_bytes=60 * 1024 * 1024
        ),
    )(*args)


def solution(mesh):
    placed = (
        P(None, "grp", "tile"),
        P(),
        P("grp", "tile"),
        P(None, "grp", "tile"),
        P(("grp", "tile"), None, None),
        P(("grp", "tile")),
        P(("grp", "tile")),
        P(("grp", "tile")),
    )
    return jax.shard_map(
        functools.partial(per_device, mesh.shape["grp"], mesh.shape["tile"]),
        mesh=mesh,
        in_specs=placed,
        out_specs=(P(None, "grp", "tile"), P(("grp", "tile"), None, None)),
        check_vma=False,
    )
```

```python
import functools
import jax
import jax.numpy as jnp
from jax import lax
from jax.experimental import pallas as pl
from jax.experimental.pallas import tpu as pltpu
from jax.sharding import PartitionSpec as P

RATIO = 8
NU = 2
NC = 4
RELAX = 0.8
HALO = 4
TOP = 16
LANES = 128
MESH = pl.DeviceIdType.MESH
HIGHEST = lax.Precision.HIGHEST
DIRECTIONS = ((-1, 0), (1, 0), (0, -1), (0, 1), (-1, -1), (-1, 1), (1, -1), (1, 1))


def inverse(x):
    r = pl.reciprocal(x, approx=True)
    return r * (2.0 - x * r)


def harmonic(a, b):
    total = a + b
    return 2.0 * a * b * inverse(jnp.where(total > 0, total, 1.0))


def guarded_weight(d):
    return RELAX * inverse(jnp.where(d > 0, d, 1.0))


def iota(shape, dim):
    return lax.broadcasted_iota(jnp.int32, shape, dim)


def shift(x, amount, axis):
    return pltpu.roll(x, amount % x.shape[axis], axis)


def rows_at(ref, l, r, offset):
    if offset < 0:
        return ref.at[l, pl.ds(pl.multiple_of(r - 8, 8), 16), :][8 + offset : 16 + offset, :]
    return ref.at[l, pl.ds(r, 16), :][offset : 8 + offset, :]


def row_sums(fields):
    shape = fields[0].shape
    row = lax.broadcasted_iota(jnp.int32, shape, 0)
    xs = list(fields) + [jnp.zeros(shape, jnp.float32)] * (8 - len(fields))

    def merge(x, y, start, run):
        first = ((row - start + 8) % 8) % (2 * run) < run
        return jnp.where(first, x, y) + shift(jnp.where(first, y, x), -run, 0)

    z = [merge(xs[j], xs[j + 4], j, 4) for j in range(4)]
    y = [merge(z[j], z[j + 2], j, 2) for j in range(2)]
    return merge(y[0], y[1], 0, 1)


def dot(a, b):
    return jnp.dot(a, b, precision=HIGHEST, preferred_element_type=jnp.float32)


def kernel(
    grp_count,
    tile_count,
    material,
    table,
    heat_sink,
    source,
    die_power,
    die_conduct,
    bond,
    place,
    out,
    die_out,
    field,
    zx,
    zy,
    zz,
    diag,
    weight,
    ua,
    ub,
    packed,
    turned,
    from_side,
    from_corner,
    sums,
    folded,
    arrived,
    rough,
    rough_side,
    rough_row,
    rough_corner,
    dies,
    die_message,
    all_dies,
    die_fix,
    all_fixes,
    wide,
    solved,
    spread,
    send_sem,
    recv_sem,
    gather_send,
    gather_recv,
):
    layers, rows, cols = material.shape
    slots, edge, _ = die_power.shape
    cell = edge // RATIO
    down, across = rows // edge, cols // edge
    crows, ccols = rows // RATIO, cols // RATIO
    width = cols + LANES
    height = rows + 2 * TOP
    n_fields = 2 * layers + 1
    area = float(RATIO * RATIO)
    per = LANES // ccols
    count = grp_count * tile_count
    g = lax.axis_index("grp")
    t = lax.axis_index("tile")
    me = g * tile_count + t

    def peer(offset):
        other = lax.rem(me + offset, count)
        return other, (other // tile_count, lax.rem(other, tile_count))

    def exists(dy, dx):
        ok = jnp.bool_(True)
        if dy:
            ok = jnp.logical_and(ok, g > 0 if dy < 0 else g < grp_count - 1)
        if dx:
            ok = jnp.logical_and(ok, t > 0 if dx < 0 else t < tile_count - 1)
        return ok

    field[:, 0:TOP, :] = jnp.zeros((n_fields, TOP, width), jnp.float32)
    field[:, height - TOP : height, :] = jnp.zeros((n_fields, TOP, width), jnp.float32)
    from_side[...] = jnp.zeros_like(from_side)
    from_corner[...] = jnp.zeros_like(from_corner)
    rough_side[...] = jnp.zeros_like(rough_side)
    rough_row[...] = jnp.zeros_like(rough_row)
    rough_corner[...] = jnp.zeros_like(rough_corner)
    zx[:, 0:8, :] = jnp.zeros((layers, 8, width), jnp.float32)

    barrier = pltpu.get_barrier_semaphore()

    @pl.loop(1, count)
    def _(offset):
        pl.semaphore_signal(barrier, inc=1, device_id=peer(offset)[1], device_id_type=MESH)

    lane8 = iota((8, LANES), 1)

    @pl.loop(0, rows // 8)
    def _(i):
        r = pl.multiple_of(i * 8, 8)
        edges = jnp.zeros((8, LANES), jnp.float32)
        summed = []
        for f in range(n_fields):
            if f < layers:
                kind = material[f, pl.ds(r, 8), :]
                values = [jnp.full((8, cols), table[m], jnp.float32) for m in range(table.shape[0])]
                bit = 1
                while len(values) > 1:
                    odd = (kind & bit) != 0
                    values = [
                        jnp.where(odd, values[m + 1], values[m]) if m + 1 < len(values) else values[m]
                        for m in range(0, len(values), 2)
                    ]
                    bit *= 2
                x = values[0]
            elif f < 2 * layers:
                x = source[f - layers, pl.ds(r, 8), :]
            else:
                x = heat_sink[pl.ds(r, 8), :]
            field[f, pl.ds(TOP + r, 8), 0:cols] = x
            if f < layers or f == 2 * layers:
                summed.append(x)
            right = shift(x[:, cols - LANES :], HALO + HALO * f, 1)
            left = shift(x[:, :LANES], 64 + HALO * f, 1)
            in_right = (lane8 >= HALO * f) & (lane8 < HALO * (f + 1))
            in_left = (lane8 >= 64 + HALO * f) & (lane8 < 64 + HALO * (f + 1))
            edges = jnp.where(in_right, right, jnp.where(in_left, left, edges))
        packed[pl.ds(r, 8), :] = edges
        sums[pl.ds(r, 8), :] = row_sums(summed)

    turned[...] = packed[...].T

    pl.semaphore_wait(barrier, count - 1)

    depth = from_side.shape[1]

    def halo_copy(k):
        dy, dx = DIRECTIONS[k]
        if dx == 0:
            src = field.at[:, pl.ds(TOP if dy < 0 else height - TOP - 8, 8), pl.ds(0, cols)]
            dst = field.at[:, pl.ds(height - TOP if dy < 0 else TOP - 8, 8), pl.ds(0, cols)]
        elif dy == 0:
            src = turned.at[pl.ds(0 if dx > 0 else 64, depth), :]
            dst = from_side.at[0 if dx > 0 else 1]
        else:
            src = packed.at[pl.ds(0 if dy < 0 else rows - 8, 8), :]
            dst = from_corner.at[k - 4]
        return pltpu.make_async_remote_copy(
            src_ref=src, dst_ref=dst, send_sem=send_sem.at[k], recv_sem=recv_sem.at[k],
            device_id=(g + dy, t + dx), device_id_type=MESH,
        )

    def rough_copy(k, phase):
        dy, dx = DIRECTIONS[k]
        half = pl.ds(2 * phase, 2)
        if dy == 0:
            src = rough.at[half]
            dst = rough_side.at[k - 2, half]
        else:
            src = rough.at[half, pl.ds(0 if dy < 0 else crows - 8, 8), :]
            dst = (rough_row.at[k, half] if dx == 0 else rough_corner.at[k - 4, half])
        s = 8 * (phase + 1) + k
        return pltpu.make_async_remote_copy(
            src_ref=src, dst_ref=dst, send_sem=send_sem.at[s], recv_sem=recv_sem.at[s],
            device_id=(g + dy, t + dx), device_id_type=MESH,
        )

    def start_all(make):
        for k, (dy, dx) in enumerate(DIRECTIONS):
            pl.when(exists(dy, dx))(lambda k=k: make(k).start())

    def wait_all_recv(make):
        for k, (dy, dx) in enumerate(DIRECTIONS):
            pl.when(exists(-dy, -dx))(lambda k=k: make(k).wait_recv())

    def wait_all_send(make):
        for k, (dy, dx) in enumerate(DIRECTIONS):
            pl.when(exists(dy, dx))(lambda k=k: make(k).wait_send())

    start_all(halo_copy)

    srow, scol = iota((edge, edge), 0), iota((edge, edge), 1)
    one, none = jnp.float32(1.0), jnp.float32(0.0)
    sides = (
        jnp.where(srow > 0, one, none) + jnp.where(srow < edge - 1, one, none)
        + jnp.where(scol > 0, one, none) + jnp.where(scol < edge - 1, one, none)
    )

    def around(v):
        return (
            jnp.where(srow > 0, shift(v, 1, 0), 0.0)
            + jnp.where(srow < edge - 1, shift(v, -1, 0), 0.0)
            + jnp.where(scol > 0, shift(v, 1, 1), 0.0)
            + jnp.where(scol < edge - 1, shift(v, -1, 1), 0.0)
        )

    rows_in = (iota((cell, edge), 0) == iota((cell, edge), 1) // RATIO).astype(jnp.float32)
    message = jnp.zeros((cell, LANES), jnp.float32)
    row_m = iota((8, LANES), 0)
    params = jnp.full((8, LANES), -1.0, jnp.float32)
    for s in range(slots):
        c, b = die_conduct[s], bond[s]
        live = jnp.where(place[s] >= 0, 1.0, 0.0)
        p = die_power[s]
        d = c * sides + b
        wt = guarded_weight(d)
        v = wt * p
        v = (1.0 - RELAX) * v + wt * (p + c * around(v))
        dies[s] = v
        resid = live * (p + c * around(v) - d * v)
        cols_in = (
            iota((edge, LANES), 0) // RATIO + cell * s == iota((edge, LANES), 1)
        ).astype(jnp.float32)
        message = message + dot(dot(rows_in, resid), cols_in)
        mine = lane8 // cell == s
        value = jnp.where(
            row_m == 0, c, jnp.where(row_m == 1, b * area, place[s].astype(jnp.float32))
        )
        params = jnp.where(mine, value, params)
    die_message[0:cell, :] = message
    die_message[cell : cell + 8, :] = params
    all_dies[me] = die_message[...]

    def gather_copy(phase, other, slot, where):
        src, dst = (die_message, all_dies) if phase == 0 else (die_fix, all_fixes)
        return pltpu.make_async_remote_copy(
            src_ref=src, dst_ref=dst.at[slot],
            send_sem=gather_send.at[phase, other], recv_sem=gather_recv.at[phase, slot],
            device_id=where, device_id_type=MESH,
        )

    def gather_start(phase):
        @pl.loop(1, count)
        def _(offset):
            other, where = peer(offset)
            gather_copy(phase, other, me, where).start()

    def gather_wait(phase):
        @pl.loop(1, count)
        def _(offset):
            other, where = peer(offset)
            gather_copy(phase, other, other, where).wait()

    gather_start(0)

    def gathered(total, first_tile):
        pick = (iota((cols, LANES), 0) // RATIO == iota((cols, LANES), 1)).astype(jnp.float32)
        folded[...] = dot(sums[...], pick)
        for tile in range(2):
            result = jnp.zeros((crows, LANES), jnp.float32)
            for q in range(per):
                f = tile * per + q
                if f < total:
                    result = result + shift(folded[pl.ds(f, crows, stride=8), :], q * ccols, 1)
            rough[first_tile + tile] = result

    gathered(layers + 1, 0)
    start_all(lambda k: rough_copy(k, 0))

    wait_all_recv(halo_copy)
    pairs = []
    for f in range(n_fields):
        pairs.append(from_side[0, HALO * f : HALO * (f + 1), :])
        pairs.append(from_side[1, HALO * f : HALO * (f + 1), :])
    pairs.append(jnp.zeros((LANES - 2 * HALO * n_fields, rows), jnp.float32))
    arrived[TOP : height - TOP, :] = jnp.concatenate(pairs, axis=0).T

    def corner(x, y):
        tile = jnp.zeros((8, LANES), jnp.float32)
        for f in range(n_fields):
            at = lane8 - 2 * HALO * f
            tile = jnp.where((at >= 0) & (at < HALO), shift(x, HALO * f, 1), tile)
            tile = jnp.where(
                (at >= HALO) & (at < 2 * HALO), shift(y, HALO * f + HALO - 64, 1), tile
            )
        return tile

    arrived[0 : TOP - 8, :] = jnp.zeros((TOP - 8, LANES), jnp.float32)
    arrived[TOP - 8 : TOP, :] = corner(from_corner[3], from_corner[2])
    arrived[height - TOP : height - TOP + 8, :] = corner(from_corner[1], from_corner[0])
    arrived[height - TOP + 8 : height, :] = jnp.zeros((TOP - 8, LANES), jnp.float32)
    in_halo = (lane8 < HALO) | (lane8 >= LANES - HALO)

    def unpack(r):
        x = arrived[pl.ds(r, 8), :]
        for f in range(n_fields):
            field[f, pl.ds(r, 8), cols:width] = jnp.where(
                in_halo, shift(x, -HALO * (2 * f + 1), 1), 0.0
            )

    unpack(8)

    @pl.loop(1, height // 8 - 1)
    def _(i):
        r = pl.multiple_of(i * 8, 8)
        unpack(pl.multiple_of(r + 8, 8))
        ks = [field[l, pl.ds(r, 8), :] for l in range(layers)]
        below = None
        for l in range(layers):
            k = ks[l]
            fx = harmonic(k, rows_at(field, l, r, 1))
            fy = harmonic(k, shift(k, -1, 1))
            zx[l, pl.ds(r, 8), :] = fx
            zy[l, pl.ds(r, 8), :] = fy
            d = fx + rows_at(zx, l, r, -1) + fy + shift(fy, 1, 1)
            if l == 0:
                d = d + field[2 * layers, pl.ds(r, 8), :]
            else:
                d = d + below
            if l < layers - 1:
                below = harmonic(k, ks[l + 1])
                zz[l, pl.ds(r, 8), :] = below
                d = d + below
            diag[l, pl.ds(r, 8), :] = d
            wt = guarded_weight(d)
            weight[l, pl.ds(r, 8), :] = wt
            ua[l, pl.ds(r, 8), :] = wt * field[layers + l, pl.ds(r, 8), :]

    def pulled(u, r, l, us):
        centre = us[l]
        fx = zx[l, pl.ds(r, 8), :]
        fy = zy[l, pl.ds(r, 8), :]
        total = field[layers + l, pl.ds(r, 8), :]
        total = total + fx * rows_at(u, l, r, 1)
        total = total + rows_at(zx, l, r, -1) * rows_at(u, l, r, -1)
        total = total + fy * shift(centre, -1, 1) + shift(fy * centre, 1, 1)
        if l > 0:
            total = total + zz[l - 1, pl.ds(r, 8), :] * us[l - 1]
        if l < layers - 1:
            total = total + zz[l, pl.ds(r, 8), :] * us[l + 1]
        return total

    def sweep(u, store, first, last):
        @pl.loop(first, last)
        def _(i):
            r = pl.multiple_of(i * 8, 8)
            us = [u[l, pl.ds(r, 8), :] for l in range(layers)]
            for l in range(layers):
                total = pulled(u, r, l, us)
                new = (1.0 - RELAX) * us[l] + weight[l, pl.ds(r, 8), :] * total
                store(l, r, new)

    def into(ref):
        def store(l, r, new):
            ref[l, pl.ds(r, 8), :] = new

        return store

    sweep(ua, into(ub), 1, height // 8 - 1)

    @pl.loop(0, crows)
    def _(i):
        r = pl.multiple_of(i * 8 + TOP, 8)
        us = [ub[l, pl.ds(r, 8), :] for l in range(layers)]
        resids = []
        for l in range(layers):
            resid = pulled(ub, r, l, us) - diag[l, pl.ds(r, 8), :] * us[l]
            resids.append(resid[:, :cols])
        sums[pl.ds(pl.multiple_of(i * 8, 8), 8), :] = row_sums(resids)

    gathered(layers, 2)
    start_all(lambda k: rough_copy(k, 1))

    gather_wait(0)
    span = tile_count * across
    chigh = crows + 16
    parts = cell + 8
    spots = [(a, b) for a in range(-1, down + 1) for b in range(-1, across + 1)]
    wanted = []
    for a, b in spots:
        pr, pc = g * down + a, t * across + b
        inside = (pr >= 0) & (pr < grp_count * down) & (pc >= 0) & (pc < span)
        wanted.append(jnp.where(inside, pr * span + pc, -2).astype(jnp.float32))

    for lo in range(0, len(spots), across + 2):

        def add(d, acc, lo=lo):
            block = all_dies[d]
            where = block[cell + 2 : cell + 3, :]
            return tuple(
                a + jnp.where(where == wanted[lo + j], block, 0.0) for j, a in enumerate(acc)
            )

        acc = lax.fori_loop(
            0, count, add, tuple(jnp.zeros((parts, LANES), jnp.float32) for _ in range(across + 2))
        )
        lane_p = iota((parts, LANES), 1)
        line = jnp.zeros((parts, LANES), jnp.float32)
        for j in range(across + 2):
            x = acc[j]
            step = LANES // 2
            while step >= cell:
                x = x + shift(x, step, 1)
                step //= 2
            line = jnp.where(lane_p // cell == j, x, line)
        line = shift(line, 8 - cell, 1)
        a = lo // (across + 2) - 1
        if a == -1:
            first, size, off = 0, 8, cell - 8
        elif a == down:
            first, size, off = 8 + crows, 8, 0
        else:
            first, size, off = 8 + a * cell, cell, 0
        n = 2 * layers + 1
        wide[n, first : first + size, :] = line[off : off + size]
        wide[n + 1, first : first + size, :] = jnp.broadcast_to(
            line[cell : cell + 1], (size, LANES)
        )
        wide[n + 2, first : first + size, :] = jnp.broadcast_to(
            line[cell + 1 : cell + 2], (size, LANES)
        )

    for phase in range(2):
        wait_all_recv(lambda k: rough_copy(k, phase))
        for f in range(layers + 1 if phase == 0 else layers):
            tile, q = 2 * phase + f // per, f % per
            target = f if phase == 0 else layers + 1 + f

            def joined(left, middle, right, size):
                lane = iota((size, LANES), 1)
                x = shift(middle, 8 - ccols * q, 1)
                x = jnp.where((lane >= 8) & (lane < 8 + ccols), x, 0.0)
                x = jnp.where(lane < 8, shift(left, 8 - ccols - ccols * q, 1), x)
                return jnp.where(
                    (lane >= 8 + ccols) & (lane < 16 + ccols),
                    shift(right, 8 + ccols - ccols * q, 1),
                    x,
                )

            wide[target, 8 : 8 + crows, :] = joined(
                rough_side[1, tile], rough[tile], rough_side[0, tile], crows
            )
            wide[target, 0:8, :] = joined(
                rough_corner[3, tile], rough_row[1, tile], rough_corner[2, tile], 8
            )
            wide[target, 8 + crows : chigh, :] = joined(
                rough_corner[1, tile], rough_row[0, tile], rough_corner[0, tile], 8
            )

    kc = [wide[l] * (1.0 / area) for l in range(layers)]
    cx = [harmonic(k, shift(k, -1, 0)) for k in kc]
    cy = [harmonic(k, shift(k, -1, 1)) for k in kc]
    cz = [harmonic(kc[l], kc[l + 1]) * area for l in range(layers - 1)]
    top_rhs, top_c, top_b = (wide[2 * layers + 1 + j] for j in range(3))
    weights = []
    for l in range(layers):
        d = cx[l] + shift(cx[l], 1, 0) + cy[l] + shift(cy[l], 1, 1)
        if l == 0:
            d = d + wide[layers]
        else:
            d = d + cz[l - 1]
        d = d + (cz[l] if l < layers - 1 else top_b)
        weights.append(guarded_weight(d))
    crow = (iota((chigh, LANES), 0) + (cell - 8)) % cell
    ccol = (iota((chigh, LANES), 1) + (cell - 8)) % cell
    low_x, high_x = crow != 0, crow != cell - 1
    low_y, high_y = ccol != 0, ccol != cell - 1
    near = sum(jnp.where(m, one, none) for m in (low_x, high_x, low_y, high_y))
    top_d = top_c * near + top_b
    top_w = guarded_weight(top_d)
    errors = [weights[l] * wide[layers + 1 + l] for l in range(layers)]
    top = top_w * top_rhs
    for _ in range(NC - 1):
        new = []
        for l in range(layers):
            e = errors[l]
            total = wide[layers + 1 + l]
            total = total + cx[l] * shift(e, -1, 0) + shift(cx[l] * e, 1, 0)
            total = total + cy[l] * shift(e, -1, 1) + shift(cy[l] * e, 1, 1)
            if l > 0:
                total = total + cz[l - 1] * errors[l - 1]
            total = total + (cz[l] * errors[l + 1] if l < layers - 1 else top_b * top)
            new.append((1.0 - RELAX) * e + weights[l] * total)
        nearby = (
            jnp.where(low_x, shift(top, 1, 0), 0.0)
            + jnp.where(high_x, shift(top, -1, 0), 0.0)
            + jnp.where(low_y, shift(top, 1, 1), 0.0)
            + jnp.where(high_y, shift(top, -1, 1), 0.0)
        )
        top = top + top_w * (
            top_rhs + top_b * errors[layers - 1] + top_c * nearby - top_d * top
        )
        errors = new
    for l in range(layers):
        solved[l] = errors[l]

    lane_c = iota((cell, LANES), 1)
    fix = jnp.zeros((cell, LANES), jnp.float32)
    for a in range(down):
        piece = shift(top[8 + a * cell : 8 + (a + 1) * cell], a * ccols - 8, 1)
        fix = jnp.where(lane_c // ccols == a, piece, fix)
    die_fix[...] = fix
    all_fixes[me] = die_fix[...]
    gather_start(1)

    column = iota((LANES, width), 1)
    source_lane = jnp.where(column < cols + LANES // 2, 8 + column // RATIO, 7)
    pick = (iota((LANES, width), 0) == source_lane).astype(jnp.float32)
    for l in range(layers):
        spread[l] = dot(solved[l], pick)

    @pl.loop(1, height // 8 - 1)
    def _(i):
        r = pl.multiple_of(i * 8, 8)
        for l in range(layers):
            ub[l, pl.ds(r, 8), :] = ub[l, pl.ds(r, 8), :] + spread[l, pl.ds(i + 6, 1), :]

    sweep(ub, into(ua), 1, height // 8 - 1)

    def finish(l, r, new):
        out[l, pl.ds(r - TOP, 8), :] = new[:, :cols]

    sweep(ua, finish, TOP // 8, (height - TOP) // 8)

    gather_wait(1)
    codes = []
    for s in range(slots):
        spot = jnp.maximum(place[s], 0)
        pr, pc = spot // span, lax.rem(spot, span)
        target = (pr // down) * tile_count + pc // across
        local = lax.rem(pr, down) * across + lax.rem(pc, across)
        codes.append(jnp.where(place[s] >= 0, target * 8 + local, -1))
    group = lane_c // cell

    def collect(d, acc):
        block = all_fixes[d]
        code = group + d * 8
        return tuple(a + jnp.where(code == codes[s], block, 0.0) for s, a in enumerate(acc))

    fixes = lax.fori_loop(
        0, count, collect, tuple(jnp.zeros((cell, LANES), jnp.float32) for _ in range(slots))
    )
    rows_out = (iota((edge, cell), 0) // RATIO == iota((edge, cell), 1)).astype(jnp.float32)
    cols_out = (iota((LANES, edge), 0) == iota((LANES, edge), 1) // RATIO).astype(jnp.float32)
    for s in range(slots):
        x = fixes[s]
        step = LANES // 2
        while step >= cell:
            x = x + shift(x, step, 1)
            step //= 2
        c, b = die_conduct[s], bond[s]
        live = jnp.where(place[s] >= 0, 1.0, 0.0)
        p = die_power[s]
        wt = guarded_weight(c * sides + b)
        v = dies[s] + live * dot(rows_out, dot(x, cols_out))
        for _ in range(NU):
            v = (1.0 - RELAX) * v + wt * (p + c * around(v))
        die_out[s] = live * v

    wait_all_send(halo_copy)
    for phase in range(2):
        wait_all_send(lambda k: rough_copy(k, phase))


def per_device(grp_count, tile_count, *args):
    material, die_power = args[0], args[4]
    layers, rows, cols = material.shape
    slots, edge, _ = die_power.shape
    cell = edge // RATIO
    crows = rows // RATIO
    width, height = cols + LANES, rows + 2 * TOP
    count = grp_count * tile_count
    n_fields = 2 * layers + 1
    depth = -(-n_fields * HALO // 8) * 8
    vmem = pl.BlockSpec(memory_space=pltpu.VMEM)
    smem = pl.BlockSpec(memory_space=pltpu.SMEM)
    f32 = jnp.float32

    def scratch(*shape):
        return pltpu.VMEM(shape, f32)

    grid = (layers, height, width)
    return pl.pallas_call(
        functools.partial(kernel, grp_count, tile_count),
        out_shape=(
            jax.ShapeDtypeStruct((layers, rows, cols), f32),
            jax.ShapeDtypeStruct((slots, edge, edge), f32),
        ),
        in_specs=[vmem, smem, vmem, vmem, vmem, smem, smem, smem],
        out_specs=(vmem, vmem),
        scratch_shapes=[
            scratch(n_fields, height, width),
            scratch(*grid),
            scratch(*grid),
            scratch(layers - 1, height, width),
            scratch(*grid),
            scratch(*grid),
            scratch(*grid),
            scratch(*grid),
            scratch(rows, LANES),
            scratch(LANES, rows),
            scratch(2, depth, rows),
            scratch(4, 8, LANES),
            scratch(rows, cols),
            scratch(rows, LANES),
            scratch(height, LANES),
            scratch(4, crows, LANES),
            scratch(2, 4, crows, LANES),
            scratch(2, 4, 8, LANES),
            scratch(4, 4, 8, LANES),
            scratch(slots, edge, edge),
            scratch(cell + 8, LANES),
            scratch(count, cell + 8, LANES),
            scratch(cell, LANES),
            scratch(count, cell, LANES),
            scratch(n_fields + 3, crows + 16, LANES),
            scratch(layers, crows + 16, LANES),
            scratch(layers, crows + 16, width),
            pltpu.SemaphoreType.DMA((24,)),
            pltpu.SemaphoreType.DMA((24,)),
            pltpu.SemaphoreType.DMA((2, count)),
            pltpu.SemaphoreType.DMA((2, count)),
        ],
        compiler_params=pltpu.CompilerParams(
            collective_id=0, has_side_effects=True, vmem_limit_bytes=47 * 1024 * 1024
        ),
    )(*args)


def solution(mesh):
    placed = (
        P(None, "grp", "tile"),
        P(),
        P("grp", "tile"),
        P(None, "grp", "tile"),
        P(("grp", "tile"), None, None),
        P(("grp", "tile")),
        P(("grp", "tile")),
        P(("grp", "tile")),
    )
    return jax.shard_map(
        functools.partial(per_device, mesh.shape["grp"], mesh.shape["tile"]),
        mesh=mesh,
        in_specs=placed,
        out_specs=(P(None, "grp", "tile"), P(("grp", "tile"), None, None)),
        check_vma=False,
    )
```
